32 devices in a mesh: ens: 2 (over y), lon: 4 (over z), lat: 2 (over x), ch: 2 (over core).
Axes of the slice: x: 2, y: 2, z: 4, core: 2. Of those that a mesh axis runs over, the one named last changes fastest.
Arguments:
- features: bfloat16 [64, 64, 256], P(('ens', 'lat'), 'lon', 'ch'), parts along dimension 0, may hold values from -6 to 6
- basis: bfloat16 [9, 32, 7, 9], replicated, may hold values from -0.8984375 to 0.8984375
- active: int32 [32, 7], replicated, may hold values from 0 to 1, as said below
- reach: int32 [32], replicated, may hold values from 1 to 4, as said below
- weight: bfloat16 [9, 256, 256], P(None, 'ch'), may hold values from -0.125 to 0.125
- cotangent: bfloat16 [64, 64, 256], P(('ens', 'lat'), 'lon', 'ch'), parts along dimension 0, may hold values from -3 to 3
Outputs:
- output: bfloat16 [64, 64, 256], P(('ens', 'lat'), 'lon', 'ch'), parts along dimension 0
- input_grad: bfloat16 [64, 64, 256], P(('ens', 'lat'), 'lon', 'ch'), parts along dimension 0
- weight_grad: float32 [18, 256, 256], P('ens', 'ch'), parts along dimension 0
The draws below stay inside these ranges and needn't reach their ends.
There are 2 independent parts, one for each index of `ens`. The reference program is written for one: setup_inputs(seed, part) draws one part's arguments, and reference() takes and returns one part's arrays. A program takes and returns all parts, laid end to end along the dimension named above; an argument that names none is the same for every part. Nothing has to cross between parts.
Inputs may be any that keep to these rules, and one draw needn't show every extreme that they name: `active`: 1 at offset 3 in every row, and at every offset in the first and last 8 rows. `reach`: equal to 4 in the first and last 8 rows.
All inputs are finite; a program needn't handle non-finite values.
Results may differ from the reference program's by a relative error of at most 0.0049.
Values may be sent and summed in bfloat16 or wider, within the bound.
A program may use at most 64 MiB of HBM per device.

```python
import jax
import jax.numpy as jnp
from jax import lax

C = 256
O = 256
K = 9
H = 3
W = 4
ROWS_DEV = 16
NLAT = 32
NLON = 64


def draw_active(key, part):
    key = jax.random.fold_in(key, 11)
    row_ids = jnp.arange(NLAT, dtype=jnp.int32)
    polar_count = ROWS_DEV // 2
    polar_rows = (row_ids < polar_count) | (row_ids >= NLAT - polar_count)
    tosses = jax.random.randint(key, (NLAT, 2 * H + 1), 0, 2)
    offsets = jnp.arange(2 * H + 1, dtype=jnp.int32)[None, :]
    centre = offsets == H
    live_mask = (tosses == 0) | polar_rows[:, None] | centre
    dead_spot = (row_ids[:, None] == NLAT // 2) & (offsets == 0)
    live_mask = live_mask & jnp.logical_not(dead_spot)
    return live_mask.astype(jnp.int32)


def draw_reach(key, part):
    key = jax.random.fold_in(key, 23)
    row_ids = jnp.arange(NLAT, dtype=jnp.int32)
    polar_count = ROWS_DEV // 2
    polar_rows = (row_ids < polar_count) | (row_ids >= NLAT - polar_count)
    base_reach = jax.random.randint(key, (NLAT,), 1, W + 1)
    base_reach = jnp.where(row_ids == NLAT // 2, 1, base_reach)
    return jnp.where(polar_rows, W, base_reach).astype(jnp.int32)


def block_scale(rng, dims, split, smallest, high):
    loudness, own = 1.0, jax.random.fold_in(rng, 6)
    for axis_at, blocks in split:
        heights = jnp.exp(jax.random.uniform(jax.random.fold_in(own, axis_at), (blocks,), jnp.float32, smallest / len(split), high / len(split)))
        loudness = loudness * jnp.repeat(heights, dims[axis_at] // blocks).reshape([-1 if axis == axis_at else 1 for axis in range(len(dims))])
    return loudness


def normal_values(own_key, dims, scale, limit, pieces=(), held_as=jnp.bfloat16):
    array = scale * jax.random.normal(own_key, dims, jnp.float32)
    if pieces:
        array = array * block_scale(own_key, dims, pieces, -0.22, 0.18)
    return jnp.clip(array, -limit, limit).astype(held_as)


def setup_inputs(seed: int = 0, part: int = 0) -> dict:
    seeds = jax.random.split(jax.random.key(seed), 7)
    part_splits = jax.random.split(jax.random.fold_in(seeds[6], part), 7)
    features = normal_values(part_splits[0], (NLAT, NLON, C), 1.0, 6.0, ((0, 2), (1, 4), (2, 2)))
    basis = normal_values(seeds[1], (K, NLAT, 2 * H + 1, 2 * W + 1), 0.15, 0.8984375)
    active = draw_active(jax.random.fold_in(seeds[6], 71), part)
    reach = draw_reach(jax.random.fold_in(seeds[6], 71), part)
    weight = normal_values(seeds[4], (K, C, O), (K * C) ** -0.5, 0.125, ((1, 2),))
    cotangent = normal_values(part_splits[5], (NLAT, NLON, O), 0.5, 3.0, ((0, 2), (1, 4), (2, 2)))
    return dict(features=features, basis=basis, active=active, reach=reach, weight=weight, cotangent=cotangent)


def masked_basis(basis, active, reach):
    distance = jnp.abs(jnp.arange(2 * W + 1, dtype=jnp.int32) - W)
    lon_live = (distance[None, :] <= reach[:, None]).astype(jnp.int32)
    live_mask = active[:, :, None] * lon_live[:, None, :]
    return basis * live_mask[None].astype(basis.dtype)


def reference(features, basis, active, reach, weight, cotangent):
    masked = masked_basis(basis, active, reach)
    padded = jnp.pad(features, ((H, H), (0, 0), (0, 0)))

    def forward_row(row_index):
        window = lax.dynamic_slice_in_dim(padded, row_index, 2 * H + 1, 0).astype(jnp.float32)
        weights_row = lax.dynamic_slice_in_dim(masked, row_index, 1, 1)[:, 0].astype(jnp.float32)
        running = jnp.zeros((NLON, K, C), jnp.float32)
        for offset in range(2 * W + 1):
            term = jnp.einsum("ka,ajc->jkc", weights_row[:, :, offset], window)
            running = running + jnp.roll(term, W - offset, axis=0)
        return running.astype(jnp.bfloat16)

    mixed = lax.map(forward_row, jnp.arange(NLAT, dtype=jnp.int32))
    flat = mixed.reshape(NLAT * NLON, K * C).astype(jnp.float32)
    flat_weight = weight.reshape(K * C, O).astype(jnp.float32)
    output = jnp.dot(flat, flat_weight, preferred_element_type=jnp.float32)
    output = output.astype(jnp.bfloat16).reshape(NLAT, NLON, O)
    flat_cot = cotangent.reshape(NLAT * NLON, O).astype(jnp.float32)
    weight_grad = jnp.dot(flat.T, flat_cot, preferred_element_type=jnp.float32).reshape(K, C, O)
    spread = jnp.dot(flat_cot, flat_weight.T, preferred_element_type=jnp.float32)
    spread = spread.astype(jnp.bfloat16).reshape(NLAT, NLON, K, C)
    spread_pad = jnp.pad(spread, ((H, H), (0, 0), (0, 0), (0, 0)))
    basis_pad = jnp.pad(masked, ((0, 0), (H, H), (0, 0), (0, 0)))

    def backward_row(row_index):
        window = lax.dynamic_slice_in_dim(spread_pad, row_index, 2 * H + 1, 0).astype(jnp.float32)
        block = lax.dynamic_slice_in_dim(basis_pad, row_index, 2 * H + 1, 1).astype(jnp.float32)
        diagonal = jnp.stack([block[:, row_lag, 2 * H - row_lag] for row_lag in range(2 * H + 1)], axis=1)
        running = jnp.zeros((NLON, C), jnp.float32)
        for offset in range(2 * W + 1):
            term = jnp.einsum("kr,rqkc->qc", diagonal[:, :, offset], window)
            running = running + jnp.roll(term, offset - W, axis=0)
        return running.astype(jnp.bfloat16)

    input_grad = lax.map(backward_row, jnp.arange(NLAT, dtype=jnp.int32))
    return (output, input_grad, weight_grad)
```

```python
import functools

import jax
import jax.numpy as jnp
from jax import lax
from jax.experimental import pallas as pl
from jax.experimental.pallas import tpu as pltpu
from jax.sharding import PartitionSpec as P

MESH = pl.DeviceIdType.MESH
QS = 32
BF = jnp.bfloat16
F32 = jnp.float32


def dot(a, b, ca, cb):
    return lax.dot_general(a, b, (((ca,), (cb,)), ((), ())), preferred_element_type=F32)


def kernel(
    dims,
    feat,
    base,
    weight,
    cot,
    out,
    igrad,
    wg,
    ext,
    acc,
    tiles,
    mixed,
    spread,
    cotf,
    pout,
    pin,
    fpk,
    edge,
    ein,
    ecorn,
    elat,
    gpk,
    gedge,
    gin,
    gcorn,
    glat,
    gf,
    gb,
    rx,
    zb,
    rz,
    zown,
    s_ch,
    r_ch,
    s_f,
    r_f,
    s_g,
    r_g,
    s_rx,
    r_rx,
    s_rz,
    r_rz,
    s_az,
    r_az,
    s_ax,
    r_ax,
):
    L, N, half, lon_half, per_lat, pc = dims
    R, J, C = feat.shape
    K = weight.shape[0]
    cells = R * J
    ens, n, l, ch = (lax.axis_index(a) for a in ("ens", "lon", "lat", "ch"))
    left, right = lax.rem(n + N - 1, N), lax.rem(n + 1, N)
    has_up, has_down = l > 0, l < L - 1

    def dev(lat, lon):
        return (ens, lon, lat, ch)

    mate = (ens, n, l, 1 - ch)
    lats = [lax.rem(l + d, L) for d in range(1, L)]
    lons = [lax.rem(n + d, N) for d in range(1, N)]

    def remote(src, dst, ss, rs, device):
        return pltpu.make_async_remote_copy(
            src_ref=src, dst_ref=dst, send_sem=ss, recv_sem=rs, device_id=device, device_id_type=MESH
        )

    barrier = pltpu.get_barrier_semaphore()

    def greet(device):
        pl.semaphore_signal(barrier, inc=1, device_id=device, device_id_type=MESH)

    greet(mate)
    for lat in lats:
        greet(dev(lat, n))
    for lon in lons:
        greet(dev(l, lon))
    for has, lat in ((has_up, l - 1), (has_down, l + 1)):

        @pl.when(has)
        def _():
            greet(dev(lat, left))
            greet(dev(lat, right))

    for r in range(R):
        row = feat[r].astype(F32)
        fpk[0, 4 * r : 4 * r + 4] = row[:lon_half]
        fpk[1, 4 * r : 4 * r + 4] = row[J - lon_half :]
    edge[...] = fpk[...].astype(BF)

    corners = 2 * (has_up.astype(jnp.int32) + has_down.astype(jnp.int32))
    pl.semaphore_wait(barrier, 1 + (L - 1) + (N - 1) + corners)

    def edge_copies(src, dst, corn_src, corn_dst, lat_src, lat_dst, ss, rs):
        def lon_copy(side):
            return remote(src(side), dst(1 - side), ss.at[side], rs.at[1 - side], dev(l, (left, right)[side]))

        def corner(side, down):
            lat = l + 1 if down else l - 1
            return remote(
                corn_src(side, down),
                corn_dst(1 - side, 1 - down),
                ss.at[2 + 2 * side + down],
                rs.at[2 + 2 * (1 - side) + (1 - down)],
                dev(lat, (left, right)[side]),
            )

        def lat_copy(down):
            lat = l + 1 if down else l - 1
            return remote(lat_src(down), lat_dst(1 - down), ss.at[6 + down], rs.at[6 + 1 - down], dev(lat, n))

        return lon_copy, corner, lat_copy

    def each(copies, action):
        lon_copy, corner, lat_copy = copies
        for side in (0, 1):
            action(lon_copy(side))
        for down, has in ((0, has_up), (1, has_down)):

            @pl.when(has)
            def _():
                action(lat_copy(down))
                for side in (0, 1):
                    action(corner(side, down))

    fwd = edge_copies(
        lambda s: edge.at[s],
        lambda s: ein.at[s],
        lambda s, d: edge.at[s, pl.ds(48 if d else 0, 16)],
        lambda s, d: ecorn.at[2 * s + d],
        lambda d: feat.at[pl.ds(R - half if d else 0, half)],
        lambda d: elat.at[d],
        s_f,
        r_f,
    )
    cot_copy = remote(cot, cotf.at[ch], s_ch.at[0], r_ch.at[0], mate)
    each(fwd, lambda c: c.start())
    cot_copy.start()

    cotf[ch] = cot[...]
    ext[...] = jnp.zeros_like(ext)
    acc[...] = jnp.zeros_like(acc)

    def make_tiles(i, _):
        for k in range(K):
            line = base[k, pl.ds(i, 1), :]
            for h in range(2):
                flat = jnp.broadcast_to(line[:, 128 * h : 128 * h + 128], (J, 128))
                turned = pltpu.roll(flat, 8 - lon_half, 1, stride=1, stride_axis=0)
                tiles[i, J * k : J * k + J, 128 * h : 128 * h + 128] = turned.astype(BF)
        return _

    lax.fori_loop(0, R, make_tiles, 0)

    for r in range(R):
        ext[r + half, 8 : 8 + J] = feat[r].astype(F32)

    def recv_wait(dst, sem):
        remote(dst, dst, sem, sem, mate).wait_recv()

    for side in (0, 1):
        recv_wait(ein.at[side], r_f.at[side])
        cols = ein[side].astype(F32)
        at = 8 - lon_half if side == 0 else 8 + J
        for r in range(R):
            ext[r + half, at : at + lon_half] = cols[4 * r : 4 * r + 4]
    for down, has in ((0, has_up), (1, has_down)):
        first = half + R if down else 0

        @pl.when(has)
        def _():
            recv_wait(elat.at[down], r_f.at[6 + down])
            for r in range(half):
                ext[first + r, 8 : 8 + J] = elat[down, r].astype(F32)
            for side in (0, 1):
                recv_wait(ecorn.at[2 * side + down], r_f.at[2 + 2 * side + down])
                cols = ecorn[2 * side + down].astype(F32)
                at = 8 - lon_half if side == 0 else 8 + J
                skip = 0 if down else 4
                for r in range(half):
                    ext[first + r, at : at + lon_half] = cols[skip + 4 * r : skip + 4 * r + 4]

    def mix(i, _):
        window = ext[pl.ds(i, 8)].reshape(8 * QS, C).astype(BF)
        row = dot(tiles[i], window, 1, 0).astype(BF)
        for k in range(K):
            mixed[k, pl.ds(pl.multiple_of(i * J, J), J)] = row[J * k : J * k + J]
        return _

    lax.fori_loop(0, R, mix, 0)

    cot_copy.wait_recv()
    cot_full = jnp.concatenate(
        [cotf[0].reshape(cells, C), cotf[1].reshape(cells, C)], axis=1
    )

    for k in range(K):
        g = dot(mixed[k], cot_full, 0, 0)
        gf[C * k : C * k + C] = g
        gb[C * k : C * k + C] = g.astype(BF)

    def rows(lat, c):
        start = lat * per_lat + jnp.minimum(c * pc, per_lat - pc)
        return pl.ds(pl.multiple_of(start, 16), pc)

    order = lons + [n]

    def rx_copy(lat, c):
        return remote(gb.at[rows(lat, c)], rx.at[l, c], s_rx.at[lat, c], r_rx.at[l, c], dev(lat, n))

    for c in order:
        for lat in lats:
            rx_copy(lat, c).start()

    def rz_copy(c):
        return remote(zb.at[c], rz.at[n], s_rz.at[c], r_rz.at[n], dev(l, c))

    def lat_sum(c):
        total = gf[rows(l, c)]
        for lat in lats:
            recv_wait(rx.at[lat, c], r_rx.at[lat, c])
            total = total + rx[lat, c].astype(F32)
        return total

    def pass_on(c):
        zb[c] = lat_sum(c).astype(BF)
        rz_copy(c).start()

    passes = list(order[:-1])

    total = dot(mixed[0], weight[0], 1, 0)
    for k in range(1, K):
        total = total + dot(mixed[k], weight[k], 1, 0)
    pout[0] = total[:, :C]
    pout[1] = total[:, C:]
    out_copy = remote(pout.at[1 - ch], pin, s_ch.at[1], r_ch.at[1], mate)
    out_copy.start()
    pass_on(passes[0])

    for k in range(K):
        part = dot(cot_full, weight[k], 1, 1).astype(BF)
        spread[:, J * k : J * k + J] = part.reshape(R, J, C)
    for c in passes[1:2]:
        pass_on(c)

    def back(i, _):
        part = dot(tiles[i], spread[i], 0, 0)
        acc[pl.ds(i, 8)] += part.reshape(8, QS, C)
        return _

    lax.fori_loop(0, R // 2, back, 0)
    for c in passes[2:3]:
        pass_on(c)
    lax.fori_loop(R // 2, R, back, 0)
    for c in passes[3:]:
        pass_on(c)
    zown[...] = lat_sum(n)

    gpk[...] = jnp.zeros_like(gpk)
    for side in (0, 1):
        at = 8 - lon_half if side == 0 else 8 + J
        for r in range(R):
            gpk[side, 4 * r : 4 * r + 4] = acc[r + half, at : at + lon_half]
        for r in range(half):
            gpk[side, 64 + 4 * r : 68 + 4 * r] = acc[r, at : at + lon_half]
            gpk[side, 80 + 4 * r : 84 + 4 * r] = acc[R + half + r, at : at + lon_half]
    gedge[...] = gpk[...].astype(BF)
    bwd = edge_copies(
        lambda s: gedge.at[s, pl.ds(0, 64)],
        lambda s: gin.at[s],
        lambda s, d: gedge.at[s, pl.ds(80 if d else 64, 16)],
        lambda s, d: gcorn.at[2 * s + d],
        lambda d: acc.at[pl.ds(R + half if d else 0, half), pl.ds(8, J)],
        lambda d: glat.at[d],
        s_g,
        r_g,
    )
    each(bwd, lambda c: c.start())

    total = zown[...]
    for c in lons:
        recv_wait(rz.at[c], r_rz.at[c])
        total = total + rz[c].astype(F32)
    wg[l, n] = total.astype(BF)

    def az_copy(lon):
        return remote(wg.at[l, n], wg.at[l, n], s_az.at[lon], r_az.at[n], dev(l, lon))

    def ax_copy(lat, c):
        return remote(wg.at[l, c], wg.at[l, c], s_ax.at[lat, c], r_ax.at[l, c], dev(lat, n))

    for lon in lons:
        az_copy(lon).start()
    for lat in lats:
        ax_copy(lat, n).start()

    out_copy.wait_recv()
    out[...] = (pout[ch] + pin[...]).astype(BF).reshape(R, J, C)

    for side in (0, 1):
        recv_wait(gin.at[side], r_g.at[side])
        cols = gin[side].astype(F32)
        at = 8 if side == 0 else 8 + J - lon_half
        for r in range(R):
            acc[r + half, at : at + lon_half] += cols[4 * r : 4 * r + 4]
    for down, has in ((0, has_up), (1, has_down)):
        first = R if down else half

        @pl.when(has)
        def _():
            recv_wait(glat.at[down], r_g.at[6 + down])
            for r in range(half):
                acc[first + r, 8 : 8 + J] += glat[down, r]
            for side in (0, 1):
                recv_wait(gcorn.at[2 * side + down], r_g.at[2 + 2 * side + down])
                cols = gcorn[2 * side + down].astype(F32)
                at = 8 if side == 0 else 8 + J - lon_half
                for r in range(half):
                    acc[first + r, at : at + lon_half] += cols[4 * r : 4 * r + 4]
    for r in range(R):
        igrad[r] = acc[r + half, 8 : 8 + J].astype(BF)

    for c in lons:
        recv_wait(wg.at[l, c], r_az.at[c])
        for lat in lats:
            ax_copy(lat, c).start()
    for c in [n] + lons:
        for lat in lats:
            recv_wait(wg.at[lat, c], r_ax.at[lat, c])

    cot_copy.wait_send()
    out_copy.wait_send()
    each(fwd, lambda c: c.wait_send())
    each(bwd, lambda c: c.wait_send())
    for c in lons:
        rz_copy(c).wait_send()
        az_copy(c).wait_send()
    for c in order:
        for lat in lats:
            rx_copy(lat, c).wait_send()
            ax_copy(lat, c).wait_send()


def live_basis(basis, active, reach, lon_half):
    distance = jnp.abs(jnp.arange(2 * lon_half + 1, dtype=jnp.int32) - lon_half)
    lon_live = (distance[None, :] <= reach[:, None]).astype(jnp.int32)
    live_mask = active[:, :, None] * lon_live[:, None, :]
    return basis * live_mask[None].astype(basis.dtype)


def body(features, basis, active, reach, weight, cotangent):
    R, J, C = features.shape
    K, _, lat_span, lon_span = basis.shape
    half, lon_half = (lat_span - 1) // 2, (lon_span - 1) // 2
    O = weight.shape[2]
    L, N = lax.axis_size("lat"), lax.axis_size("lon")
    per_lat = K * C // L
    pc = -(-per_lat // (16 * N)) * 16
    cells = R * J

    first = lax.axis_index("lat") * R
    own = lax.dynamic_slice_in_dim(basis, first, R, 1)
    own = live_basis(
        own,
        lax.dynamic_slice_in_dim(active, first, R, 0),
        lax.dynamic_slice_in_dim(reach, first, R, 0),
        lon_half,
    ).astype(F32)
    base = jnp.pad(own, ((0, 0), (0, 0), (0, 8 - lat_span), (0, QS - lon_span)))
    base = base.reshape(K, R, 8 * QS)

    vmem = pl.BlockSpec(memory_space=pltpu.VMEM)
    dma = pltpu.SemaphoreType.DMA
    output, input_grad, wg = pl.pallas_call(
        functools.partial(kernel, (L, N, half, lon_half, per_lat, pc)),
        out_shape=(
            jax.ShapeDtypeStruct((R, J, C), BF),
            jax.ShapeDtypeStruct((R, J, C), BF),
            jax.ShapeDtypeStruct((L, N, pc, O), BF),
        ),
        in_specs=[vmem] * 4,
        out_specs=(vmem,) * 3,
        scratch_shapes=[
            pltpu.VMEM((R + 8, QS, C), F32),
            pltpu.VMEM((R + 8, QS, C), F32),
            pltpu.VMEM((R, K * J, 8 * QS), BF),
            pltpu.VMEM((K, cells, C), BF),
            pltpu.VMEM((R, K * J, C), BF),
            pltpu.VMEM((2, R, J, C), BF),
            pltpu.VMEM((2, cells, C), F32),
            pltpu.VMEM((cells, C), F32),
            pltpu.VMEM((2, 64, C), F32),
            pltpu.VMEM((2, 64, C), BF),
            pltpu.VMEM((2, 64, C), BF),
            pltpu.VMEM((4, 16, C), BF),
            pltpu.VMEM((2, half, J, C), BF),
            pltpu.VMEM((2, 96, C), F32),
            pltpu.VMEM((2, 96, C), BF),
            pltpu.VMEM((2, 64, C), BF),
            pltpu.VMEM((4, 16, C), BF),
            pltpu.VMEM((2, half, J, C), F32),
            pltpu.VMEM((K * C, O), F32),
            pltpu.VMEM((K * C, O), BF),
            pltpu.VMEM((L, N, pc, O), BF),
            pltpu.VMEM((N, pc, O), BF),
            pltpu.VMEM((N, pc, O), BF),
            pltpu.VMEM((pc, O), F32),
            dma((2,)),
            dma((2,)),
            dma((8,)),
            dma((8,)),
            dma((8,)),
            dma((8,)),
            dma((L, N)),
            dma((L, N)),
            dma((N,)),
            dma((N,)),
            dma((N,)),
            dma((N,)),
            dma((L, N)),
            dma((L, N)),
        ],
        compiler_params=pltpu.CompilerParams(
            collective_id=0, has_side_effects=True, vmem_limit_bytes=40 * 1024 * 1024
        ),
    )(features, base, weight, cotangent)
    weight_grad = wg.reshape(L, N * pc, O)[:, :per_lat].reshape(K, C, O).astype(F32)
    return output, input_grad, weight_grad


def solution(mesh):
    return jax.shard_map(
        body,
        mesh=mesh,
        in_specs=(
            P(("ens", "lat"), "lon", "ch"),
            P(),
            P(),
            P(),
            P(None, "ch", None),
            P(("ens", "lat"), "lon", "ch"),
        ),
        out_specs=(
            P(("ens", "lat"), "lon", "ch"),
            P(("ens", "lat"), "lon", "ch"),
            P("ens", "ch", None),
        ),
        check_vma=False,
    )
```

```python
import functools

import jax
import jax.numpy as jnp
from jax import lax
from jax.experimental import pallas as pl
from jax.experimental.pallas import tpu as pltpu
from jax.sharding import PartitionSpec as P

MESH = pl.DeviceIdType.MESH
QS = 32
BF = jnp.bfloat16
F32 = jnp.float32


def dot(a, b, ca, cb):
    return lax.dot_general(a, b, (((ca,), (cb,)), ((), ())), preferred_element_type=F32)


def kernel(
    dims,
    feat,
    basis,
    active,
    reach,
    weight,
    cot,
    out,
    igrad,
    wg,
    base,
    ext,
    acc,
    tiles,
    mixed,
    spread,
    cotf,
    pout,
    pin,
    fpk,
    edge,
    ein,
    ecorn,
    elat,
    gpk,
    gedge,
    gin,
    gcorn,
    glat,
    gf,
    gb,
    rx,
    zb,
    rz,
    zown,
    s_ch,
    r_ch,
    s_f,
    r_f,
    s_g,
    r_g,
    s_rx,
    r_rx,
    s_rz,
    r_rz,
    s_az,
    r_az,
    s_ax,
    r_ax,
):
    L, N, half, lon_half, per_lat, pc = dims
    R, J, C = feat.shape
    K = weight.shape[0]
    cells = R * J
    ens, n, l, ch = (lax.axis_index(a) for a in ("ens", "lon", "lat", "ch"))
    left, right = lax.rem(n + N - 1, N), lax.rem(n + 1, N)
    has_up, has_down = l > 0, l < L - 1

    def dev(lat, lon):
        return (ens, lon, lat, ch)

    mate = (ens, n, l, 1 - ch)
    lats = [lax.rem(l + d, L) for d in range(1, L)]
    lons = [lax.rem(n + d, N) for d in range(1, N)]

    def remote(src, dst, ss, rs, device):
        return pltpu.make_async_remote_copy(
            src_ref=src, dst_ref=dst, send_sem=ss, recv_sem=rs, device_id=device, device_id_type=MESH
        )

    barrier = pltpu.get_barrier_semaphore()

    def greet(device):
        pl.semaphore_signal(barrier, inc=1, device_id=device, device_id_type=MESH)

    greet(mate)
    for lat in lats:
        greet(dev(lat, n))
    for lon in lons:
        greet(dev(l, lon))
    for has, lat in ((has_up, l - 1), (has_down, l + 1)):

        @pl.when(has)
        def _():
            greet(dev(lat, left))
            greet(dev(lat, right))

    for r in range(R):
        row = feat[r].astype(F32)
        fpk[0, 4 * r : 4 * r + 4] = row[:lon_half]
        fpk[1, 4 * r : 4 * r + 4] = row[J - lon_half :]
    edge[...] = fpk[...].astype(BF)

    A, B = basis.shape[2], basis.shape[1]
    where = lax.broadcasted_iota(jnp.int32, (8 * B, 8 * QS), 0)
    lane = lax.broadcasted_iota(jnp.int32, (8 * B, 8 * QS), 1)
    place = (lane == (where % 8) * QS + where // 8).astype(F32).astype(BF)
    live = active[...]
    far = reach[...]
    blank = jnp.zeros((8 - A, live.shape[1]), F32)
    lives = [(live * (abs(b - lon_half) <= far).astype(jnp.int32)).astype(F32) for b in range(B)]
    for k in range(K):
        planes = []
        for b in range(B):
            planes += [basis[k, b].astype(F32) * lives[b], blank]
        base[k] = dot(jnp.concatenate(planes, axis=0).astype(BF), place, 0, 0)

    def make_tiles(i, _):
        for k in range(K):
            line = base[k, pl.ds(l * R + i, 1), :]
            for h in range(2):
                flat = jnp.broadcast_to(line[:, 128 * h : 128 * h + 128], (J, 128))
                turned = pltpu.roll(flat, 8 - lon_half, 1, stride=1, stride_axis=0)
                tiles[i, J * k : J * k + J, 128 * h : 128 * h + 128] = turned.astype(BF)
        return _

    lax.fori_loop(0, R, make_tiles, 0, unroll=4)

    cotf[ch] = cot[...]
    ext[...] = jnp.zeros_like(ext)
    acc[...] = jnp.zeros_like(acc)

    for r in range(R):
        ext[r + half, 8 : 8 + J] = feat[r].astype(F32)

    corners = 2 * (has_up.astype(jnp.int32) + has_down.astype(jnp.int32))
    pl.semaphore_wait(barrier, 1 + (L - 1) + (N - 1) + corners)

    def edge_copies(src, dst, corn_src, corn_dst, lat_src, lat_dst, ss, rs):
        def lon_copy(side):
            return remote(src(side), dst(1 - side), ss.at[side], rs.at[1 - side], dev(l, (left, right)[side]))

        def corner(side, down):
            lat = l + 1 if down else l - 1
            return remote(
                corn_src(side, down),
                corn_dst(1 - side, 1 - down),
                ss.at[2 + 2 * side + down],
                rs.at[2 + 2 * (1 - side) + (1 - down)],
                dev(lat, (left, right)[side]),
            )

        def lat_copy(down):
            lat = l + 1 if down else l - 1
            return remote(lat_src(down), lat_dst(1 - down), ss.at[6 + down], rs.at[6 + 1 - down], dev(lat, n))

        return lon_copy, corner, lat_copy

    def each(copies, action):
        lon_copy, corner, lat_copy = copies
        for side in (0, 1):
            action(lon_copy(side))
        for down, has in ((0, has_up), (1, has_down)):

            @pl.when(has)
            def _():
                action(lat_copy(down))
                for side in (0, 1):
                    action(corner(side, down))

    fwd = edge_copies(
        lambda s: edge.at[s],
        lambda s: ein.at[s],
        lambda s, d: edge.at[s, pl.ds(48 if d else 0, 16)],
        lambda s, d: ecorn.at[2 * s + d],
        lambda d: feat.at[pl.ds(R - half if d else 0, half)],
        lambda d: elat.at[d],
        s_f,
        r_f,
    )
    cot_copy = remote(cot, cotf.at[ch], s_ch.at[0], r_ch.at[0], mate)
    each(fwd, lambda c: c.start())
    cot_copy.start()

    def recv_wait(dst, sem):
        remote(dst, dst, sem, sem, mate).wait_recv()

    cot_copy.wait_recv()
    cot_full = jnp.concatenate(
        [cotf[0].reshape(cells, C), cotf[1].reshape(cells, C)], axis=1
    )

    for k in range(K):
        part = dot(cot_full, weight[k], 1, 1).astype(BF)
        spread[:, J * k : J * k + J] = part.reshape(R, J, C)

    def back(i, _):
        part = dot(tiles[i], spread[i], 0, 0)
        acc[pl.ds(i, 8)] += part.reshape(8, QS, C)
        return _

    lax.fori_loop(0, R // 2, back, 0, unroll=4)

    for side in (0, 1):
        recv_wait(ein.at[side], r_f.at[side])
        cols = ein[side].astype(F32)
        at = 8 - lon_half if side == 0 else 8 + J
        for r in range(R):
            ext[r + half, at : at + lon_half] = cols[4 * r : 4 * r + 4]
    for down, has in ((0, has_up), (1, has_down)):
        first = half + R if down else 0

        @pl.when(has)
        def _():
            recv_wait(elat.at[down], r_f.at[6 + down])
            for r in range(half):
                ext[first + r, 8 : 8 + J] = elat[down, r].astype(F32)
            for side in (0, 1):
                recv_wait(ecorn.at[2 * side + down], r_f.at[2 + 2 * side + down])
                cols = ecorn[2 * side + down].astype(F32)
                at = 8 - lon_half if side == 0 else 8 + J
                skip = 0 if down else 4
                for r in range(half):
                    ext[first + r, at : at + lon_half] = cols[skip + 4 * r : skip + 4 * r + 4]

    def mix(i, _):
        window = ext[pl.ds(i, 8)].reshape(8 * QS, C).astype(BF)
        row = dot(tiles[i], window, 1, 0).astype(BF)
        for k in range(K):
            mixed[k, pl.ds(pl.multiple_of(i * J, J), J)] = row[J * k : J * k + J]
        return _

    lax.fori_loop(0, R, mix, 0, unroll=4)

    for k in range(K):
        g = dot(mixed[k], cot_full, 0, 0)
        gf[C * k : C * k + C] = g
        gb[C * k : C * k + C] = g.astype(BF)

    def rows(lat, c):
        start = lat * per_lat + jnp.minimum(c * pc, per_lat - pc)
        return pl.ds(pl.multiple_of(start, 16), pc)

    order = lons + [n]

    def rx_copy(lat, c):
        return remote(gb.at[rows(lat, c)], rx.at[l, c], s_rx.at[lat, c], r_rx.at[l, c], dev(lat, n))

    for c in order:
        for lat in lats:
            rx_copy(lat, c).start()

    def rz_copy(c):
        return remote(zb.at[c], rz.at[n], s_rz.at[c], r_rz.at[n], dev(l, c))

    def lat_sum(c):
        total = gf[rows(l, c)]
        for lat in lats:
            recv_wait(rx.at[lat, c], r_rx.at[lat, c])
            total = total + rx[lat, c].astype(F32)
        return total

    def pass_on(c):
        zb[c] = lat_sum(c).astype(BF)
        rz_copy(c).start()

    total = dot(mixed[0], weight[0], 1, 0)
    for k in range(1, K):
        total = total + dot(mixed[k], weight[k], 1, 0)
    pout[0] = total[:, :C]
    pout[1] = total[:, C:]
    out_copy = remote(pout.at[1 - ch], pin, s_ch.at[1], r_ch.at[1], mate)
    out_copy.start()

    lax.fori_loop(R // 2, R, back, 0, unroll=4)

    gpk[...] = jnp.zeros_like(gpk)
    for side in (0, 1):
        at = 8 - lon_half if side == 0 else 8 + J
        for r in range(R):
            gpk[side, 4 * r : 4 * r + 4] = acc[r + half, at : at + lon_half]
        for r in range(half):
            gpk[side, 64 + 4 * r : 68 + 4 * r] = acc[r, at : at + lon_half]
            gpk[side, 80 + 4 * r : 84 + 4 * r] = acc[R + half + r, at : at + lon_half]
    gedge[...] = gpk[...].astype(BF)
    bwd = edge_copies(
        lambda s: gedge.at[s, pl.ds(0, 64)],
        lambda s: gin.at[s],
        lambda s, d: gedge.at[s, pl.ds(80 if d else 64, 16)],
        lambda s, d: gcorn.at[2 * s + d],
        lambda d: acc.at[pl.ds(R + half if d else 0, half), pl.ds(8, J)],
        lambda d: glat.at[d],
        s_g,
        r_g,
    )
    each(bwd, lambda c: c.start())

    for c in lons:
        pass_on(c)
    zown[...] = lat_sum(n)

    total = zown[...]
    for c in lons:
        recv_wait(rz.at[c], r_rz.at[c])
        total = total + rz[c].astype(F32)
    wg[l, n] = total.astype(BF)

    def az_copy(lon):
        return remote(wg.at[l, n], wg.at[l, n], s_az.at[lon], r_az.at[n], dev(l, lon))

    def ax_copy(lat, c):
        return remote(wg.at[l, c], wg.at[l, c], s_ax.at[lat, c], r_ax.at[l, c], dev(lat, n))

    for lon in lons:
        az_copy(lon).start()
    for lat in lats:
        ax_copy(lat, n).start()

    out_copy.wait_recv()
    out[...] = (pout[ch] + pin[...]).astype(BF).reshape(R, J, C)

    for side in (0, 1):
        recv_wait(gin.at[side], r_g.at[side])
        cols = gin[side].astype(F32)
        at = 8 if side == 0 else 8 + J - lon_half
        for r in range(R):
            acc[r + half, at : at + lon_half] += cols[4 * r : 4 * r + 4]
    for down, has in ((0, has_up), (1, has_down)):
        first = R if down else half

        @pl.when(has)
        def _():
            recv_wait(glat.at[down], r_g.at[6 + down])
            for r in range(half):
                acc[first + r, 8 : 8 + J] += glat[down, r]
            for side in (0, 1):
                recv_wait(gcorn.at[2 * side + down], r_g.at[2 + 2 * side + down])
                cols = gcorn[2 * side + down].astype(F32)
                at = 8 if side == 0 else 8 + J - lon_half
                for r in range(half):
                    acc[first + r, at : at + lon_half] += cols[4 * r : 4 * r + 4]
    for r in range(R):
        igrad[r] = acc[r + half, 8 : 8 + J].astype(BF)

    for c in lons:
        recv_wait(wg.at[l, c], r_az.at[c])
        for lat in lats:
            ax_copy(lat, c).start()
    for c in [n] + lons:
        for lat in lats:
            recv_wait(wg.at[lat, c], r_ax.at[lat, c])

    cot_copy.wait_send()
    out_copy.wait_send()
    each(fwd, lambda c: c.wait_send())
    each(bwd, lambda c: c.wait_send())
    for c in lons:
        rz_copy(c).wait_send()
        az_copy(c).wait_send()
    for c in order:
        for lat in lats:
            rx_copy(lat, c).wait_send()
            ax_copy(lat, c).wait_send()


def body(features, basis, active, reach, weight, cotangent):
    R, J, C = features.shape
    K, rows, lat_span, lon_span = basis.shape
    half, lon_half = (lat_span - 1) // 2, (lon_span - 1) // 2
    O = weight.shape[2]
    L, N = lax.axis_size("lat"), lax.axis_size("lon")
    per_lat = K * C // L
    pc = -(-per_lat // (16 * N)) * 16
    cells = R * J

    vmem = pl.BlockSpec(memory_space=pltpu.VMEM)
    dma = pltpu.SemaphoreType.DMA
    output, input_grad, wg = pl.pallas_call(
        functools.partial(kernel, (L, N, half, lon_half, per_lat, pc)),
        out_shape=(
            jax.ShapeDtypeStruct((R, J, C), BF),
            jax.ShapeDtypeStruct((R, J, C), BF),
            jax.ShapeDtypeStruct((L, N, pc, O), BF),
        ),
        in_specs=[vmem] * 6,
        out_specs=(vmem,) * 3,
        scratch_shapes=[
            pltpu.VMEM((K, rows, 8 * QS), F32),
            pltpu.VMEM((R + 8, QS, C), F32),
            pltpu.VMEM((R + 8, QS, C), F32),
            pltpu.VMEM((R, K * J, 8 * QS), BF),
            pltpu.VMEM((K, cells, C), BF),
            pltpu.VMEM((R, K * J, C), BF),
            pltpu.VMEM((2, R, J, C), BF),
            pltpu.VMEM((2, cells, C), F32),
            pltpu.VMEM((cells, C), F32),
            pltpu.VMEM((2, 64, C), F32),
            pltpu.VMEM((2, 64, C), BF),
            pltpu.VMEM((2, 64, C), BF),
            pltpu.VMEM((4, 16, C), BF),
            pltpu.VMEM((2, half, J, C), BF),
            pltpu.VMEM((2, 96, C), F32),
            pltpu.VMEM((2, 96, C), BF),
            pltpu.VMEM((2, 64, C), BF),
            pltpu.VMEM((4, 16, C), BF),
            pltpu.VMEM((2, half, J, C), F32),
            pltpu.VMEM((K * C, O), F32),
            pltpu.VMEM((K * C, O), BF),
            pltpu.VMEM((L, N, pc, O), BF),
            pltpu.VMEM((N, pc, O), BF),
            pltpu.VMEM((N, pc, O), BF),
            pltpu.VMEM((pc, O), F32),
            dma((2,)),
            dma((2,)),
            dma((8,)),
            dma((8,)),
            dma((8,)),
            dma((8,)),
            dma((L, N)),
            dma((L, N)),
            dma((N,)),
            dma((N,)),
            dma((N,)),
            dma((N,)),
            dma((L, N)),
            dma((L, N)),
        ],
        compiler_params=pltpu.CompilerParams(
            collective_id=0, has_side_effects=True, vmem_limit_bytes=40 * 1024 * 1024
        ),
    )(
        features,
        basis.transpose(0, 3, 2, 1),
        active.T,
        reach.reshape(1, -1),
        weight,
        cotangent,
    )
    weight_grad = wg.reshape(L, N * pc, O)[:, :per_lat].reshape(K, C, O).astype(F32)
    return output, input_grad, weight_grad


def solution(mesh):
    return jax.shard_map(
        body,
        mesh=mesh,
        in_specs=(
            P(("ens", "lat"), "lon", "ch"),
            P(),
            P(),
            P(),
            P(None, "ch", None),
            P(("ens", "lat"), "lon", "ch"),
        ),
        out_specs=(
            P(("ens", "lat"), "lon", "ch"),
            P(("ens", "lat"), "lon", "ch"),
            P("ens", "ch", None),
        ),
        check_vma=False,
    )
```

```python
import functools

import jax
import jax.numpy as jnp
from jax import lax
from jax.experimental import pallas as pl
from jax.experimental.pallas import tpu as pltpu
from jax.sharding import PartitionSpec as P

MESH = pl.DeviceIdType.MESH
QS = 32
BF = jnp.bfloat16
F32 = jnp.float32
GRANT = 63 * 1024 * 1024


def dot(a, b, ca, cb):
    return lax.dot_general(a, b, (((ca,), (cb,)), ((), ())), preferred_element_type=F32)


def kernel(
    dims,
    feat_hbm,
    basis_hbm,
    active_hbm,
    reach_hbm,
    weight_hbm,
    cot_hbm,
    out_hbm,
    igrad_hbm,
    wg_hbm,
    out,
    igrad,
    wg,
    s_out,
    feat,
    basis,
    active,
    reach,
    weight,
    cot,
    s_in,
    base,
    ext,
    acc,
    tiles,
    mixed,
    spread,
    cotf,
    pout,
    pin,
    fpk,
    edge,
    ein,
    ecorn,
    elat,
    gpk,
    gedge,
    gin,
    gcorn,
    glat,
    gf,
    gb,
    rx,
    zb,
    rz,
    zown,
    s_ch,
    r_ch,
    s_f,
    r_f,
    s_g,
    r_g,
    s_rx,
    r_rx,
    s_rz,
    r_rz,
    s_az,
    r_az,
    s_ax,
    r_ax,
):
    L, N, half, lon_half, per_lat, pc = dims
    R, J, C = feat.shape
    K = weight.shape[0]
    cells = R * J
    ens, n, l, ch = (lax.axis_index(a) for a in ("ens", "lon", "lat", "ch"))
    left, right = lax.rem(n + N - 1, N), lax.rem(n + 1, N)
    has_up, has_down = l > 0, l < L - 1

    def dev(lat, lon):
        return (ens, lon, lat, ch)

    mate = (ens, n, l, 1 - ch)
    lats = [lax.rem(l + d, L) for d in range(1, L)]
    low = n < N // 2
    lons = []
    for step in range(N - 1):
        down, up = N - 1 - step, step
        down = jnp.where(down <= n, down - 1, down)
        up = jnp.where(up >= n, up + 1, up)
        lons.append(jnp.where(low, down, up))

    def remote(src, dst, ss, rs, device):
        return pltpu.make_async_remote_copy(
            src_ref=src, dst_ref=dst, send_sem=ss, recv_sem=rs, device_id=device, device_id_type=MESH
        )

    barrier = pltpu.get_barrier_semaphore()

    def greet(device):
        pl.semaphore_signal(barrier, inc=1, device_id=device, device_id_type=MESH)

    greet(mate)
    for lat in lats:
        greet(dev(lat, n))
    for lon in lons:
        greet(dev(l, lon))
    for has, lat in ((has_up, l - 1), (has_down, l + 1)):

        @pl.when(has)
        def _():
            greet(dev(lat, left))
            greet(dev(lat, right))

    pairs = (
        (feat_hbm, feat),
        (cot_hbm, cot),
        (basis_hbm, basis),
        (active_hbm, active),
        (reach_hbm, reach),
        (weight_hbm, weight),
    )
    loads = [pltpu.make_async_copy(src, dst, s_in.at[i]) for i, (src, dst) in enumerate(pairs)]
    for load in loads:
        load.start()
    loads[0].wait()

    for r in range(R):
        row = feat[r].astype(F32)
        fpk[0, 4 * r : 4 * r + 4] = row[:lon_half]
        fpk[1, 4 * r : 4 * r + 4] = row[J - lon_half :]
    edge[...] = fpk[...].astype(BF)

    for load in loads[2:5]:
        load.wait()

    A, B = basis.shape[2], basis.shape[1]
    where = lax.broadcasted_iota(jnp.int32, (8 * B, 8 * QS), 0)
    lane = lax.broadcasted_iota(jnp.int32, (8 * B, 8 * QS), 1)
    place = (lane == (where % 8) * QS + where // 8).astype(F32).astype(BF)
    live = active[...]
    far = reach[...]
    blank = jnp.zeros((8 - A, live.shape[1]), F32)
    lives = [(live * (abs(b - lon_half) <= far).astype(jnp.int32)).astype(F32) for b in range(B)]
    for k in range(K):
        planes = []
        for b in range(B):
            planes += [basis[k, b].astype(F32) * lives[b], blank]
        base[k] = dot(jnp.concatenate(planes, axis=0).astype(BF), place, 0, 0)

    def make_tiles(i, _):
        for k in range(K):
            line = base[k, pl.ds(l * R + i, 1), :]
            for h in range(2):
                flat = jnp.broadcast_to(line[:, 128 * h : 128 * h + 128], (J, 128))
                turned = pltpu.roll(flat, 8 - lon_half, 1, stride=1, stride_axis=0)
                tiles[i, J * k : J * k + J, 128 * h : 128 * h + 128] = turned.astype(BF)
        return _

    lax.fori_loop(0, R, make_tiles, 0, unroll=4)

    ext[...] = jnp.zeros_like(ext)
    acc[...] = jnp.zeros_like(acc)
    for r in range(R):
        ext[r + half, 8 : 8 + J] = feat[r].astype(F32)


    corners = 2 * (has_up.astype(jnp.int32) + has_down.astype(jnp.int32))
    pl.semaphore_wait(barrier, 1 + (L - 1) + (N - 1) + corners)

    def edge_copies(src, dst, corn_src, corn_dst, lat_src, lat_dst, ss, rs):
        def lon_copy(side):
            return remote(src(side), dst(1 - side), ss.at[side], rs.at[1 - side], dev(l, (left, right)[side]))

        def corner(side, down):
            lat = l + 1 if down else l - 1
            return remote(
                corn_src(side, down),
                corn_dst(1 - side, 1 - down),
                ss.at[2 + 2 * side + down],
                rs.at[2 + 2 * (1 - side) + (1 - down)],
                dev(lat, (left, right)[side]),
            )

        def lat_copy(down):
            lat = l + 1 if down else l - 1
            return remote(lat_src(down), lat_dst(1 - down), ss.at[6 + down], rs.at[6 + 1 - down], dev(lat, n))

        return lon_copy, corner, lat_copy

    def each(copies, action):
        lon_copy, corner, lat_copy = copies
        for side in (0, 1):
            action(lon_copy(side))
        for down, has in ((0, has_up), (1, has_down)):

            @pl.when(has)
            def _():
                action(lat_copy(down))
                for side in (0, 1):
                    action(corner(side, down))

    fwd = edge_copies(
        lambda s: edge.at[s],
        lambda s: ein.at[s],
        lambda s, d: edge.at[s, pl.ds(48 if d else 0, 16)],
        lambda s, d: ecorn.at[2 * s + d],
        lambda d: feat.at[pl.ds(R - half if d else 0, half)],
        lambda d: elat.at[d],
        s_f,
        r_f,
    )
    loads[1].wait()
    cot_copy = remote(cot, cotf.at[ch], s_ch.at[0], r_ch.at[0], mate)
    each(fwd, lambda c: c.start())
    cot_copy.start()
    cotf[ch] = cot[...]

    def recv_wait(dst, sem):
        remote(dst, dst, sem, sem, mate).wait_recv()

    loads[5].wait()
    cot_copy.wait_recv()
    cot_full = jnp.concatenate(
        [cotf[0].reshape(cells, C), cotf[1].reshape(cells, C)], axis=1
    )

    for k in range(K):
        part = dot(cot_full, weight[k], 1, 1).astype(BF)
        spread[:, J * k : J * k + J] = part.reshape(R, J, C)

    def back(i, _):
        part = dot(tiles[i], spread[i], 0, 0)
        acc[pl.ds(i, 8)] += part.reshape(8, QS, C)
        return _

    for side in (0, 1):
        recv_wait(ein.at[side], r_f.at[side])
        cols = ein[side].astype(F32)
        at = 8 - lon_half if side == 0 else 8 + J
        for r in range(R):
            ext[r + half, at : at + lon_half] = cols[4 * r : 4 * r + 4]
    for down, has in ((0, has_up), (1, has_down)):
        first = half + R if down else 0

        @pl.when(has)
        def _():
            recv_wait(elat.at[down], r_f.at[6 + down])
            for r in range(half):
                ext[first + r, 8 : 8 + J] = elat[down, r].astype(F32)
            for side in (0, 1):
                recv_wait(ecorn.at[2 * side + down], r_f.at[2 + 2 * side + down])
                cols = ecorn[2 * side + down].astype(F32)
                at = 8 - lon_half if side == 0 else 8 + J
                skip = 0 if down else 4
                for r in range(half):
                    ext[first + r, at : at + lon_half] = cols[skip + 4 * r : skip + 4 * r + 4]

    def mix(i, _):
        window = ext[pl.ds(i, 8)].reshape(8 * QS, C).astype(BF)
        row = dot(tiles[i], window, 1, 0).astype(BF)
        for k in range(K):
            mixed[k, pl.ds(pl.multiple_of(i * J, J), J)] = row[J * k : J * k + J]
        return _

    lax.fori_loop(0, R, mix, 0, unroll=4)

    for k in range(K):
        g = dot(mixed[k], cot_full, 0, 0)
        gf[C * k : C * k + C] = g
        gb[C * k : C * k + C] = g.astype(BF)

    def rows(lat, c):
        start = lat * per_lat + jnp.minimum(c * pc, per_lat - pc)
        return pl.ds(pl.multiple_of(start, 16), pc)

    order = lons + [n]

    def rx_copy(lat, c):
        return remote(gb.at[rows(lat, c)], rx.at[l, c], s_rx.at[lat, c], r_rx.at[l, c], dev(lat, n))

    for c in order:
        for lat in lats:
            rx_copy(lat, c).start()

    def rz_copy(c):
        return remote(zb.at[c], rz.at[n], s_rz.at[c], r_rz.at[n], dev(l, c))

    def lat_sum(c):
        total = gf[rows(l, c)]
        for lat in lats:
            recv_wait(rx.at[lat, c], r_rx.at[lat, c])
            total = total + rx[lat, c].astype(F32)
        return total

    def pass_on(c):
        zb[c] = lat_sum(c).astype(BF)
        rz_copy(c).start()

    total = dot(mixed[0], weight[0], 1, 0)
    for k in range(1, K):
        total = total + dot(mixed[k], weight[k], 1, 0)
    pout[0] = total[:, :C]
    pout[1] = total[:, C:]
    out_copy = remote(pout.at[1 - ch], pin, s_ch.at[1], r_ch.at[1], mate)
    out_copy.start()

    lax.fori_loop(0, R // 2, back, 0, unroll=4)
    pass_on(lons[0])
    lax.fori_loop(R // 2, R, back, 0, unroll=4)
    for c in lons[1:2]:
        pass_on(c)

    gpk[...] = jnp.zeros_like(gpk)
    for side in (0, 1):
        at = 8 - lon_half if side == 0 else 8 + J
        for r in range(R):
            gpk[side, 4 * r : 4 * r + 4] = acc[r + half, at : at + lon_half]
        for r in range(half):
            gpk[side, 64 + 4 * r : 68 + 4 * r] = acc[r, at : at + lon_half]
            gpk[side, 80 + 4 * r : 84 + 4 * r] = acc[R + half + r, at : at + lon_half]
    gedge[...] = gpk[...].astype(BF)
    bwd = edge_copies(
        lambda s: gedge.at[s, pl.ds(0, 64)],
        lambda s: gin.at[s],
        lambda s, d: gedge.at[s, pl.ds(80 if d else 64, 16)],
        lambda s, d: gcorn.at[2 * s + d],
        lambda d: acc.at[pl.ds(R + half if d else 0, half), pl.ds(8, J)],
        lambda d: glat.at[d],
        s_g,
        r_g,
    )
    each(bwd, lambda c: c.start())

    for c in lons[2:]:
        pass_on(c)
    zown[...] = lat_sum(n)

    total = zown[...]
    for c in lons:
        recv_wait(rz.at[c], r_rz.at[c])
        total = total + rz[c].astype(F32)
    wg[l, n] = total.astype(BF)

    def az_copy(lon):
        return remote(wg.at[l, n], wg.at[l, n], s_az.at[lon], r_az.at[n], dev(l, lon))

    def ax_copy(lat, c):
        return remote(wg.at[l, c], wg.at[l, c], s_ax.at[lat, c], r_ax.at[l, c], dev(lat, n))

    for lon in lons:
        az_copy(lon).start()
    for lat in lats:
        ax_copy(lat, n).start()

    out_copy.wait_recv()
    out[...] = (pout[ch] + pin[...]).astype(BF).reshape(R, J, C)
    results = [pltpu.make_async_copy(out, out_hbm, s_out.at[0])]
    results[-1].start()

    for side in (0, 1):
        recv_wait(gin.at[side], r_g.at[side])
        cols = gin[side].astype(F32)
        at = 8 if side == 0 else 8 + J - lon_half
        for r in range(R):
            acc[r + half, at : at + lon_half] += cols[4 * r : 4 * r + 4]
    for down, has in ((0, has_up), (1, has_down)):
        first = R if down else half

        @pl.when(has)
        def _():
            recv_wait(glat.at[down], r_g.at[6 + down])
            for r in range(half):
                acc[first + r, 8 : 8 + J] += glat[down, r]
            for side in (0, 1):
                recv_wait(gcorn.at[2 * side + down], r_g.at[2 + 2 * side + down])
                cols = gcorn[2 * side + down].astype(F32)
                at = 8 if side == 0 else 8 + J - lon_half
                for r in range(half):
                    acc[first + r, at : at + lon_half] += cols[4 * r : 4 * r + 4]
    for r in range(R):
        igrad[r] = acc[r + half, 8 : 8 + J].astype(BF)
    results.append(pltpu.make_async_copy(igrad, igrad_hbm, s_out.at[1]))
    results[-1].start()

    def chunk_out(lat, c, at):
        results.append(pltpu.make_async_copy(wg.at[lat, c], wg_hbm.at[lat, c], s_out.at[at]))
        results[-1].start()

    chunk_out(l, n, 2)

    near = lons[::-1]
    for i, c in enumerate(near):
        recv_wait(wg.at[l, c], r_az.at[c])
        for lat in lats:
            ax_copy(lat, c).start()
        chunk_out(l, c, 3 + i)
    for i, c in enumerate([n] + near):
        for j, lat in enumerate(lats):
            recv_wait(wg.at[lat, c], r_ax.at[lat, c])
            chunk_out(lat, c, 2 + N + (L - 1) * i + j)

    for result in results:
        result.wait()
    cot_copy.wait_send()
    out_copy.wait_send()
    each(fwd, lambda c: c.wait_send())
    each(bwd, lambda c: c.wait_send())
    for c in lons:
        rz_copy(c).wait_send()
        az_copy(c).wait_send()
    for c in order:
        for lat in lats:
            rx_copy(lat, c).wait_send()
            ax_copy(lat, c).wait_send()


def body(features, basis, active, reach, weight, cotangent):
    R, J, C = features.shape
    K, rows, lat_span, lon_span = basis.shape
    half, lon_half = (lat_span - 1) // 2, (lon_span - 1) // 2
    O = weight.shape[2]
    L, N = lax.axis_size("lat"), lax.axis_size("lon")
    per_lat = K * C // L
    pc = -(-per_lat // (16 * N)) * 16
    cells = R * J

    dma = pltpu.SemaphoreType.DMA
    output, input_grad, wg = pl.pallas_call(
        functools.partial(kernel, (L, N, half, lon_half, per_lat, pc)),
        out_shape=(
            jax.ShapeDtypeStruct((R, J, C), BF),
            jax.ShapeDtypeStruct((R, J, C), BF),
            jax.ShapeDtypeStruct((L, N, pc, O), BF),
        ),
        in_specs=[pl.BlockSpec(memory_space=pltpu.HBM)] * 6,
        out_specs=(pl.BlockSpec(memory_space=pltpu.HBM),) * 3,
        scratch_shapes=[
            pltpu.VMEM((R, J, C), BF),
            pltpu.VMEM((R, J, C), BF),
            pltpu.VMEM((L, N, pc, O), BF),
            dma((2 + L * N,)),
            pltpu.VMEM((R, J, C), BF),
            pltpu.VMEM((K, lon_span, lat_span, rows), BF),
            pltpu.VMEM((lat_span, rows), jnp.int32),
            pltpu.VMEM((1, rows), jnp.int32),
            pltpu.VMEM((K, C, O), BF),
            pltpu.VMEM((R, J, C), BF),
            dma((6,)),
            pltpu.VMEM((K, rows, 8 * QS), F32),
            pltpu.VMEM((R + 8, QS, C), F32),
            pltpu.VMEM((R + 8, QS, C), F32),
            pltpu.VMEM((R, K * J, 8 * QS), BF),
            pltpu.VMEM((K, cells, C), BF),
            pltpu.VMEM((R, K * J, C), BF),
            pltpu.VMEM((2, R, J, C), BF),
            pltpu.VMEM((2, cells, C), F32),
            pltpu.VMEM((cells, C), F32),
            pltpu.VMEM((2, 64, C), F32),
            pltpu.VMEM((2, 64, C), BF),
            pltpu.VMEM((2, 64, C), BF),
            pltpu.VMEM((4, 16, C), BF),
            pltpu.VMEM((2, half, J, C), BF),
            pltpu.VMEM((2, 96, C), F32),
            pltpu.VMEM((2, 96, C), BF),
            pltpu.VMEM((2, 64, C), BF),
            pltpu.VMEM((4, 16, C), BF),
            pltpu.VMEM((2, half, J, C), F32),
            pltpu.VMEM((K * C, O), F32),
            pltpu.VMEM((K * C, O), BF),
            pltpu.VMEM((L, N, pc, O), BF),
            pltpu.VMEM((N, pc, O), BF),
            pltpu.VMEM((N, pc, O), BF),
            pltpu.VMEM((pc, O), F32),
            dma((2,)),
            dma((2,)),
            dma((8,)),
            dma((8,)),
            dma((8,)),
            dma((8,)),
            dma((L, N)),
            dma((L, N)),
            dma((N,)),
            dma((N,)),
            dma((N,)),
            dma((N,)),
            dma((L, N)),
            dma((L, N)),
        ],
        compiler_params=pltpu.CompilerParams(
            collective_id=0, has_side_effects=True, vmem_limit_bytes=GRANT
        ),
    )(
        features,
        basis.transpose(0, 3, 2, 1),
        active.T,
        reach.reshape(1, -1),
        weight,
        cotangent,
    )
    weight_grad = wg.reshape(L, N * pc, O)[:, :per_lat].reshape(K, C, O).astype(F32)
    return output, input_grad, weight_grad


def solution(mesh):
    return jax.shard_map(
        body,
        mesh=mesh,
        in_specs=(
            P(("ens", "lat"), "lon", "ch"),
            P(),
            P(),
            P(),
            P(None, "ch", None),
            P(("ens", "lat"), "lon", "ch"),
        ),
        out_specs=(
            P(("ens", "lat"), "lon", "ch"),
            P(("ens", "lat"), "lon", "ch"),
            P("ens", "ch", None),
        ),
        check_vma=False,
    )
```

```python
import functools

import jax
import jax.numpy as jnp
from jax import lax
from jax.experimental import pallas as pl
from jax.experimental.pallas import tpu as pltpu
from jax.sharding import PartitionSpec as P

MESH = pl.DeviceIdType.MESH
QS = 32
BF = jnp.bfloat16
F32 = jnp.float32
GRANT = 63 * 1024 * 1024


def dot(a, b, ca, cb):
    return lax.dot_general(a, b, (((ca,), (cb,)), ((), ())), preferred_element_type=F32)


def kernel(
    dims,
    feat_hbm,
    basis_hbm,
    active_hbm,
    reach_hbm,
    weight_hbm,
    cot_hbm,
    out_hbm,
    igrad_hbm,
    wg_hbm,
    out,
    igrad,
    wg,
    s_out,
    feat,
    basis,
    active,
    reach,
    weight,
    cot,
    s_in,
    base,
    ext,
    extb,
    acc,
    tiles,
    mixed,
    spread,
    cotf,
    pout,
    pin,
    fpk,
    edge,
    ein,
    ecorn,
    elat,
    gpk,
    gedge,
    gin,
    gcorn,
    glat,
    gf,
    gb,
    rx,
    zb,
    rz,
    zown,
    s_ch,
    r_ch,
    s_f,
    r_f,
    s_g,
    r_g,
    s_rx,
    r_rx,
    s_rz,
    r_rz,
    s_az,
    r_az,
    s_ax,
    r_ax,
):
    L, N, half, lon_half, per_lat, pc = dims
    R, J, C = feat.shape
    K = weight.shape[0]
    cells = R * J
    ens, n, l, ch = (lax.axis_index(a) for a in ("ens", "lon", "lat", "ch"))
    left, right = lax.rem(n + N - 1, N), lax.rem(n + 1, N)
    has_up, has_down = l > 0, l < L - 1

    def dev(lat, lon):
        return (ens, lon, lat, ch)

    mate = (ens, n, l, 1 - ch)
    lats = [lax.rem(l + d, L) for d in range(1, L)]
    low = n < N // 2
    lons = []
    for step in range(N - 1):
        down, up = N - 1 - step, step
        down = jnp.where(down <= n, down - 1, down)
        up = jnp.where(up >= n, up + 1, up)
        lons.append(jnp.where(low, down, up))

    def remote(src, dst, ss, rs, device):
        return pltpu.make_async_remote_copy(
            src_ref=src, dst_ref=dst, send_sem=ss, recv_sem=rs, device_id=device, device_id_type=MESH
        )

    barrier = pltpu.get_barrier_semaphore()

    def greet(device):
        pl.semaphore_signal(barrier, inc=1, device_id=device, device_id_type=MESH)

    for has, lat in ((has_up, l - 1), (has_down, l + 1)):

        @pl.when(has)
        def _():
            greet(dev(lat, left))
            greet(dev(lat, right))

    for lon in lons:
        greet(dev(l, lon))
    for lat in lats:
        greet(dev(lat, n))
    greet(mate)

    pairs = (
        (feat_hbm, feat),
        (cot_hbm, cot),
        (basis_hbm, basis),
        (active_hbm, active),
        (reach_hbm, reach),
        (weight_hbm, weight),
    )
    loads = [pltpu.make_async_copy(src, dst, s_in.at[i]) for i, (src, dst) in enumerate(pairs)]
    for load in loads:
        load.start()
    loads[0].wait()

    for r in range(R):
        row = feat[r].astype(F32)
        fpk[0, 4 * r : 4 * r + 4] = row[:lon_half]
        fpk[1, 4 * r : 4 * r + 4] = row[J - lon_half :]
    edge[...] = fpk[...].astype(BF)

    for load in loads[2:5]:
        load.wait()

    A, B = basis.shape[2], basis.shape[1]
    where = lax.broadcasted_iota(jnp.int32, (8 * B, 8 * QS), 0)
    lane = lax.broadcasted_iota(jnp.int32, (8 * B, 8 * QS), 1)
    place = (lane == (where % 8) * QS + where // 8).astype(F32).astype(BF)
    live = active[...]
    far = reach[...]
    blank = jnp.zeros((8 - A, live.shape[1]), F32)
    lives = [(live * (abs(b - lon_half) <= far).astype(jnp.int32)).astype(F32) for b in range(B)]
    for k in range(K):
        planes = []
        for b in range(B):
            planes += [basis[k, b].astype(F32) * lives[b], blank]
        base[k] = dot(jnp.concatenate(planes, axis=0).astype(BF), place, 0, 0)

    def make_tiles(i, _):
        for k in range(K):
            line = base[k, pl.ds(l * R + i, 1), :]
            for h in range(2):
                flat = jnp.broadcast_to(line[:, 128 * h : 128 * h + 128], (J, 128))
                turned = pltpu.roll(flat, 8 - lon_half, 1, stride=1, stride_axis=0)
                tiles[i, J * k : J * k + J, 128 * h : 128 * h + 128] = turned.astype(BF)
        return _

    lax.fori_loop(0, R, make_tiles, 0, unroll=4)

    ext[...] = jnp.zeros_like(ext)
    acc[...] = jnp.zeros_like(acc)
    for r in range(R):
        ext[r + half, 8 : 8 + J] = feat[r].astype(F32)


    corners = 2 * (has_up.astype(jnp.int32) + has_down.astype(jnp.int32))
    pl.semaphore_wait(barrier, 1 + (L - 1) + (N - 1) + corners)

    def edge_copies(src, dst, corn_src, corn_dst, lat_src, lat_dst, ss, rs):
        def lon_copy(side):
            return remote(src(side), dst(1 - side), ss.at[side], rs.at[1 - side], dev(l, (left, right)[side]))

        def corner(side, down):
            lat = l + 1 if down else l - 1
            return remote(
                corn_src(side, down),
                corn_dst(1 - side, 1 - down),
                ss.at[2 + 2 * side + down],
                rs.at[2 + 2 * (1 - side) + (1 - down)],
                dev(lat, (left, right)[side]),
            )

        def lat_copy(down):
            lat = l + 1 if down else l - 1
            return remote(lat_src(down), lat_dst(1 - down), ss.at[6 + down], rs.at[6 + 1 - down], dev(lat, n))

        return lon_copy, corner, lat_copy

    def each(copies, action):
        lon_copy, corner, lat_copy = copies
        for down, has in ((0, has_up), (1, has_down)):

            @pl.when(has)
            def _():
                for side in (0, 1):
                    action(corner(side, down))

        for side in (0, 1):
            action(lon_copy(side))
        for down, has in ((0, has_up), (1, has_down)):

            @pl.when(has)
            def _():
                action(lat_copy(down))

    fwd = edge_copies(
        lambda s: edge.at[s],
        lambda s: ein.at[s],
        lambda s, d: edge.at[s, pl.ds(48 if d else 0, 16)],
        lambda s, d: ecorn.at[2 * s + d],
        lambda d: feat.at[pl.ds(R - half if d else 0, half)],
        lambda d: elat.at[d],
        s_f,
        r_f,
    )
    loads[1].wait()
    cot_copy = remote(cot, cotf.at[ch], s_ch.at[0], r_ch.at[0], mate)
    each(fwd, lambda c: c.start())
    cot_copy.start()
    cotf[ch] = cot[...]

    def recv_wait(dst, sem):
        remote(dst, dst, sem, sem, mate).wait_recv()

    loads[5].wait()
    cot_copy.wait_recv()
    cot_full = jnp.concatenate(
        [cotf[0].reshape(cells, C), cotf[1].reshape(cells, C)], axis=1
    )

    for k in range(K):
        part = dot(cot_full, weight[k], 1, 1).astype(BF)
        spread[:, J * k : J * k + J] = part.reshape(R, J, C)

    def back(i, _):
        part = dot(tiles[i], spread[i], 0, 0)
        acc[pl.ds(i, 8)] += part.reshape(8, QS, C)
        return _

    lax.fori_loop(0, R // 2, back, 0, unroll=4)

    for side in (0, 1):
        recv_wait(ein.at[side], r_f.at[side])
        cols = ein[side].astype(F32)
        at = 8 - lon_half if side == 0 else 8 + J
        for r in range(R):
            ext[r + half, at : at + lon_half] = cols[4 * r : 4 * r + 4]
    for down, has in ((0, has_up), (1, has_down)):
        first = half + R if down else 0

        @pl.when(has)
        def _():
            recv_wait(elat.at[down], r_f.at[6 + down])
            for r in range(half):
                ext[first + r, 8 : 8 + J] = elat[down, r].astype(F32)
            for side in (0, 1):
                recv_wait(ecorn.at[2 * side + down], r_f.at[2 + 2 * side + down])
                cols = ecorn[2 * side + down].astype(F32)
                at = 8 - lon_half if side == 0 else 8 + J
                skip = 0 if down else 4
                for r in range(half):
                    ext[first + r, at : at + lon_half] = cols[skip + 4 * r : skip + 4 * r + 4]

    extb[...] = ext[...].astype(BF)

    def mix(i, _):
        window = extb[pl.ds(i, 8)].reshape(8 * QS, C)
        row = dot(tiles[i], window, 1, 0).astype(BF)
        for k in range(K):
            mixed[k, pl.ds(pl.multiple_of(i * J, J), J)] = row[J * k : J * k + J]
        return _

    lax.fori_loop(0, R, mix, 0, unroll=4)

    start_k = (lats + [l])[0] * per_lat // C

    def grad(step):
        k = lax.rem(start_k + step, K)
        g = dot(mixed[k], cot_full, 0, 0)
        at = pl.ds(pl.multiple_of(k * C, C), C)
        gf[at] = g
        gb[at] = g.astype(BF)

    head = -(-per_lat // C) + (0 if per_lat % C == 0 or L == 2 else 1)
    for step in range(head):
        grad(step)

    cut = -(-pc // 32) * 16
    pieces = [(0, cut), (cut, pc - cut)] if pc > cut else [(0, pc)]

    def part(p):
        return pl.ds(pieces[p][0], pieces[p][1])

    def rows(lat, c, p):
        start = lat * per_lat + jnp.minimum(c * pc, per_lat - pc) + pieces[p][0]
        return pl.ds(pl.multiple_of(start, 16), pieces[p][1])

    P2 = range(len(pieces))

    order = lons + [n]

    def rx_copy(lat, c, p):
        return remote(
            gb.at[rows(lat, c, p)], rx.at[l, c, part(p)], s_rx.at[lat, c, p], r_rx.at[l, c, p], dev(lat, n)
        )

    for c in order:
        for lat in lats[:1]:
            for p in P2:
                rx_copy(lat, c, p).start()
    for step in range(head, K):
        grad(step)
    for c in order:
        for lat in lats[1:]:
            for p in P2:
                rx_copy(lat, c, p).start()

    def rz_copy(c, p):
        return remote(zb.at[c, part(p)], rz.at[n, part(p)], s_rz.at[c, p], r_rz.at[n, p], dev(l, c))

    def lat_sum(c, p):
        total = gf[rows(l, c, p)]
        for lat in lats:
            recv_wait(rx.at[lat, c, part(p)], r_rx.at[lat, c, p])
            total = total + rx[lat, c, part(p)].astype(F32)
        return total

    def pass_on(c):
        for p in P2:
            zb[c, part(p)] = lat_sum(c, p).astype(BF)
            rz_copy(c, p).start()

    total = dot(mixed[0], weight[0], 1, 0)
    for k in range(1, K):
        total = total + dot(mixed[k], weight[k], 1, 0)
    pout[0] = total[:, :C]
    pout[1] = total[:, C:]
    out_copy = remote(pout.at[1 - ch], pin, s_ch.at[1], r_ch.at[1], mate)
    out_copy.start()

    lax.fori_loop(R // 2, R, back, 0, unroll=4)

    gpk[...] = jnp.zeros_like(gpk)
    for side in (0, 1):
        at = 8 - lon_half if side == 0 else 8 + J
        for r in range(R):
            gpk[side, 4 * r : 4 * r + 4] = acc[r + half, at : at + lon_half]
        for r in range(half):
            gpk[side, 64 + 4 * r : 68 + 4 * r] = acc[r, at : at + lon_half]
            gpk[side, 80 + 4 * r : 84 + 4 * r] = acc[R + half + r, at : at + lon_half]
    gedge[...] = gpk[...].astype(BF)
    bwd = edge_copies(
        lambda s: gedge.at[s, pl.ds(0, 64)],
        lambda s: gin.at[s],
        lambda s, d: gedge.at[s, pl.ds(80 if d else 64, 16)],
        lambda s, d: gcorn.at[2 * s + d],
        lambda d: acc.at[pl.ds(R + half if d else 0, half), pl.ds(8, J)],
        lambda d: glat.at[d],
        s_g,
        r_g,
    )
    each(bwd, lambda c: c.start())

    for c in lons:
        pass_on(c)
    for p in P2:
        zown[part(p)] = lat_sum(n, p)

    def az_copy(lon, p):
        here = wg.at[l, n, part(p)]
        return remote(here, here, s_az.at[lon, p], r_az.at[n, p], dev(l, lon))

    def ax_copy(lat, c, p):
        return remote(
            wg.at[l, c, part(p)], wg_hbm.at[l, c, part(p)], s_ax.at[lat, c, p], r_ax.at[l, c, p], dev(lat, n)
        )

    for p in P2:
        total = zown[part(p)]
        for c in lons[::-1]:
            recv_wait(rz.at[c, part(p)], r_rz.at[c, p])
            total = total + rz[c, part(p)].astype(F32)
        wg[l, n, part(p)] = total.astype(BF)
        for lon in lons:
            az_copy(lon, p).start()
        for lat in lats:
            ax_copy(lat, n, p).start()

    out_copy.wait_recv()
    out[...] = (pout[ch] + pin[...]).astype(BF).reshape(R, J, C)
    results = [pltpu.make_async_copy(out, out_hbm, s_out.at[0])]
    results[-1].start()

    for side in (0, 1):
        recv_wait(gin.at[side], r_g.at[side])
        cols = gin[side].astype(F32)
        at = 8 if side == 0 else 8 + J - lon_half
        for r in range(R):
            acc[r + half, at : at + lon_half] += cols[4 * r : 4 * r + 4]
    for down, has in ((0, has_up), (1, has_down)):
        first = R if down else half

        @pl.when(has)
        def _():
            recv_wait(glat.at[down], r_g.at[6 + down])
            for r in range(half):
                acc[first + r, 8 : 8 + J] += glat[down, r]
            for side in (0, 1):
                recv_wait(gcorn.at[2 * side + down], r_g.at[2 + 2 * side + down])
                cols = gcorn[2 * side + down].astype(F32)
                at = 8 if side == 0 else 8 + J - lon_half
                for r in range(half):
                    acc[first + r, at : at + lon_half] += cols[4 * r : 4 * r + 4]
    for r in range(R):
        igrad[r] = acc[r + half, 8 : 8 + J].astype(BF)
    results.append(pltpu.make_async_copy(igrad, igrad_hbm, s_out.at[1]))
    results[-1].start()

    def chunk_out(lat, c, at):
        results.append(pltpu.make_async_copy(wg.at[lat, c], wg_hbm.at[lat, c], s_out.at[at]))
        results[-1].start()

    chunk_out(l, n, 2)

    near = lons[::-1]
    for i, c in enumerate(near):
        for p in P2:
            recv_wait(wg.at[l, c, part(p)], r_az.at[c, p])
            for lat in lats:
                ax_copy(lat, c, p).start()
        chunk_out(l, c, 3 + i)
    for c in [n] + near:
        for lat in lats:
            for p in P2:
                recv_wait(wg_hbm.at[lat, c, part(p)], r_ax.at[lat, c, p])

    for result in results:
        result.wait()
    cot_copy.wait_send()
    out_copy.wait_send()
    each(fwd, lambda c: c.wait_send())
    each(bwd, lambda c: c.wait_send())
    for c in lons:
        for p in P2:
            rz_copy(c, p).wait_send()
            az_copy(c, p).wait_send()
    for c in order:
        for lat in lats:
            for p in P2:
                rx_copy(lat, c, p).wait_send()
                ax_copy(lat, c, p).wait_send()


def body(features, basis, active, reach, weight, cotangent):
    R, J, C = features.shape
    K, rows, lat_span, lon_span = basis.shape
    half, lon_half = (lat_span - 1) // 2, (lon_span - 1) // 2
    O = weight.shape[2]
    L, N = lax.axis_size("lat"), lax.axis_size("lon")
    per_lat = K * C // L
    pc = -(-per_lat // (16 * N)) * 16
    cells = R * J

    dma = pltpu.SemaphoreType.DMA
    output, input_grad, wg = pl.pallas_call(
        functools.partial(kernel, (L, N, half, lon_half, per_lat, pc)),
        out_shape=(
            jax.ShapeDtypeStruct((R, J, C), BF),
            jax.ShapeDtypeStruct((R, J, C), BF),
            jax.ShapeDtypeStruct((L, N, pc, O), BF),
        ),
        in_specs=[pl.BlockSpec(memory_space=pltpu.HBM)] * 6,
        out_specs=(pl.BlockSpec(memory_space=pltpu.HBM),) * 3,
        scratch_shapes=[
            pltpu.VMEM((R, J, C), BF),
            pltpu.VMEM((R, J, C), BF),
            pltpu.VMEM((L, N, pc, O), BF),
            dma((2 + N,)),
            pltpu.VMEM((R, J, C), BF),
            pltpu.VMEM((K, lon_span, lat_span, rows), BF),
            pltpu.VMEM((lat_span, rows), jnp.int32),
            pltpu.VMEM((1, rows), jnp.int32),
            pltpu.VMEM((K, C, O), BF),
            pltpu.VMEM((R, J, C), BF),
            dma((6,)),
            pltpu.VMEM((K, rows, 8 * QS), F32),
            pltpu.VMEM((R + 8, QS, C), F32),
            pltpu.VMEM((R + 8, QS, C), BF),
            pltpu.VMEM((R + 8, QS, C), F32),
            pltpu.VMEM((R, K * J, 8 * QS), BF),
            pltpu.VMEM((K, cells, C), BF),
            pltpu.VMEM((R, K * J, C), BF),
            pltpu.VMEM((2, R, J, C), BF),
            pltpu.VMEM((2, cells, C), F32),
            pltpu.VMEM((cells, C), F32),
            pltpu.VMEM((2, 64, C), F32),
            pltpu.VMEM((2, 64, C), BF),
            pltpu.VMEM((2, 64, C), BF),
            pltpu.VMEM((4, 16, C), BF),
            pltpu.VMEM((2, half, J, C), BF),
            pltpu.VMEM((2, 96, C), F32),
            pltpu.VMEM((2, 96, C), BF),
            pltpu.VMEM((2, 64, C), BF),
            pltpu.VMEM((4, 16, C), BF),
            pltpu.VMEM((2, half, J, C), F32),
            pltpu.VMEM((K * C, O), F32),
            pltpu.VMEM((K * C, O), BF),
            pltpu.VMEM((L, N, pc, O), BF),
            pltpu.VMEM((N, pc, O), BF),
            pltpu.VMEM((N, pc, O), BF),
            pltpu.VMEM((pc, O), F32),
            dma((2,)),
            dma((2,)),
            dma((8,)),
            dma((8,)),
            dma((8,)),
            dma((8,)),
            dma((L, N, 2)),
            dma((L, N, 2)),
            dma((N, 2)),
            dma((N, 2)),
            dma((N, 2)),
            dma((N, 2)),
            dma((L, N, 2)),
            dma((L, N, 2)),
        ],
        compiler_params=pltpu.CompilerParams(
            collective_id=0, has_side_effects=True, vmem_limit_bytes=GRANT
        ),
    )(
        features,
        basis.transpose(0, 3, 2, 1),
        active.T,
        reach.reshape(1, -1),
        weight,
        cotangent,
    )
    weight_grad = wg.reshape(L, N * pc, O)[:, :per_lat].reshape(K, C, O).astype(F32)
    return output, input_grad, weight_grad


def solution(mesh):
    return jax.shard_map(
        body,
        mesh=mesh,
        in_specs=(
            P(("ens", "lat"), "lon", "ch"),
            P(),
            P(),
            P(),
            P(None, "ch", None),
            P(("ens", "lat"), "lon", "ch"),
        ),
        out_specs=(
            P(("ens", "lat"), "lon", "ch"),
            P(("ens", "lat"), "lon", "ch"),
            P("ens", "ch", None),
        ),
        check_vma=False,
    )
```

```python
import functools

import jax
import jax.numpy as jnp
from jax import lax
from jax.experimental import pallas as pl
from jax.experimental.pallas import tpu as pltpu
from jax.sharding import PartitionSpec as P

MESH = pl.DeviceIdType.MESH
QS = 32
BF = jnp.bfloat16
F32 = jnp.float32
GRANT = 63 * 1024 * 1024


def dot(a, b, ca, cb):
    return lax.dot_general(a, b, (((ca,), (cb,)), ((), ())), preferred_element_type=F32)


def kernel(
    dims,
    feat_hbm,
    basis_hbm,
    active_hbm,
    reach_hbm,
    weight_hbm,
    cot_hbm,
    out_hbm,
    igrad_hbm,
    wg_hbm,
    out,
    igrad,
    wg,
    s_out,
    feat,
    basis,
    active,
    reach,
    weight,
    cot,
    s_in,
    base,
    ext,
    extb,
    acc,
    tiles,
    mixed,
    spread,
    cotf,
    pout,
    pin,
    fpk,
    edge,
    ein,
    ecorn,
    elat,
    gpk,
    gedge,
    gin,
    gcorn,
    glat,
    gf,
    gb,
    rx,
    zb,
    rz,
    zown,
    s_ch,
    r_ch,
    s_f,
    r_f,
    s_g,
    r_g,
    s_rx,
    r_rx,
    s_rz,
    r_rz,
    s_az,
    r_az,
    s_ax,
    r_ax,
):
    L, N, half, lon_half, per_lat, pc = dims
    R, J, C = feat.shape
    K = weight.shape[0]
    cells = R * J
    ens, n, l, ch = (lax.axis_index(a) for a in ("ens", "lon", "lat", "ch"))
    left, right = lax.rem(n + N - 1, N), lax.rem(n + 1, N)
    has_up, has_down = l > 0, l < L - 1

    def dev(lat, lon):
        return (ens, lon, lat, ch)

    mate = (ens, n, l, 1 - ch)
    lats = [lax.rem(l + d, L) for d in range(1, L)]
    low = n < N // 2
    lons = []
    for step in range(N - 1):
        down, up = N - 1 - step, step
        down = jnp.where(down <= n, down - 1, down)
        up = jnp.where(up >= n, up + 1, up)
        lons.append(jnp.where(low, down, up))

    def remote(src, dst, ss, rs, device):
        return pltpu.make_async_remote_copy(
            src_ref=src, dst_ref=dst, send_sem=ss, recv_sem=rs, device_id=device, device_id_type=MESH
        )

    barrier = pltpu.get_barrier_semaphore()

    def greet(device):
        pl.semaphore_signal(barrier, inc=1, device_id=device, device_id_type=MESH)

    for has, lat in ((has_up, l - 1), (has_down, l + 1)):

        @pl.when(has)
        def _():
            greet(dev(lat, left))
            greet(dev(lat, right))

    for lon in lons:
        greet(dev(l, lon))
    for lat in lats:
        greet(dev(lat, n))
    greet(mate)

    pairs = (
        (feat_hbm, feat),
        (cot_hbm, cot),
        (basis_hbm, basis),
        (active_hbm, active),
        (reach_hbm, reach),
        (weight_hbm, weight),
    )
    loads = [pltpu.make_async_copy(src, dst, s_in.at[i]) for i, (src, dst) in enumerate(pairs)]
    for load in loads:
        load.start()
    loads[0].wait()

    for r in range(R):
        row = feat[r].astype(F32)
        fpk[0, 4 * r : 4 * r + 4] = row[:lon_half]
        fpk[1, 4 * r : 4 * r + 4] = row[J - lon_half :]
    edge[...] = fpk[...].astype(BF)

    for load in loads[2:5]:
        load.wait()

    A, B = basis.shape[2], basis.shape[1]
    where = lax.broadcasted_iota(jnp.int32, (8 * B, 8 * QS), 0)
    lane = lax.broadcasted_iota(jnp.int32, (8 * B, 8 * QS), 1)
    place = (lane == (where % 8) * QS + where // 8).astype(F32).astype(BF)
    live = active[...]
    far = reach[...]
    blank = jnp.zeros((8 - A, live.shape[1]), F32)
    lives = [(live * (abs(b - lon_half) <= far).astype(jnp.int32)).astype(F32) for b in range(B)]
    for k in range(K):
        planes = []
        for b in range(B):
            planes += [basis[k, b].astype(F32) * lives[b], blank]
        base[k] = dot(jnp.concatenate(planes, axis=0).astype(BF), place, 0, 0)

    def make_tiles(i, _):
        for k in range(K):
            line = base[k, pl.ds(l * R + i, 1), :]
            for h in range(2):
                flat = jnp.broadcast_to(line[:, 128 * h : 128 * h + 128], (J, 128))
                turned = pltpu.roll(flat, 8 - lon_half, 1, stride=1, stride_axis=0)
                tiles[i, J * k : J * k + J, 128 * h : 128 * h + 128] = turned.astype(BF)
        return _

    lax.fori_loop(0, R, make_tiles, 0, unroll=8)

    ext[...] = jnp.zeros_like(ext)
    acc[...] = jnp.zeros_like(acc)
    for r in range(R):
        ext[r + half, 8 : 8 + J] = feat[r].astype(F32)


    corners = 2 * (has_up.astype(jnp.int32) + has_down.astype(jnp.int32))
    pl.semaphore_wait(barrier, 1 + (L - 1) + (N - 1) + corners)

    def edge_copies(src, dst, corn_src, corn_dst, lat_src, lat_dst, ss, rs):
        def lon_copy(side):
            return remote(src(side), dst(1 - side), ss.at[side], rs.at[1 - side], dev(l, (left, right)[side]))

        def corner(side, down):
            lat = l + 1 if down else l - 1
            return remote(
                corn_src(side, down),
                corn_dst(1 - side, 1 - down),
                ss.at[2 + 2 * side + down],
                rs.at[2 + 2 * (1 - side) + (1 - down)],
                dev(lat, (left, right)[side]),
            )

        def lat_copy(down):
            lat = l + 1 if down else l - 1
            return remote(lat_src(down), lat_dst(1 - down), ss.at[6 + down], rs.at[6 + 1 - down], dev(lat, n))

        return lon_copy, corner, lat_copy

    def each(copies, action):
        lon_copy, corner, lat_copy = copies
        for down, has in ((0, has_up), (1, has_down)):

            @pl.when(has)
            def _():
                for side in (0, 1):
                    action(corner(side, down))

        for side in (0, 1):
            action(lon_copy(side))
        for down, has in ((0, has_up), (1, has_down)):

            @pl.when(has)
            def _():
                action(lat_copy(down))

    fwd = edge_copies(
        lambda s: edge.at[s],
        lambda s: ein.at[s],
        lambda s, d: edge.at[s, pl.ds(48 if d else 0, 16)],
        lambda s, d: ecorn.at[2 * s + d],
        lambda d: feat.at[pl.ds(R - half if d else 0, half)],
        lambda d: elat.at[d],
        s_f,
        r_f,
    )
    loads[1].wait()
    cot_copy = remote(cot, cotf.at[ch], s_ch.at[0], r_ch.at[0], mate)
    each(fwd, lambda c: c.start())
    cot_copy.start()
    cotf[ch] = cot[...]

    def recv_wait(dst, sem):
        remote(dst, dst, sem, sem, mate).wait_recv()

    loads[5].wait()
    cot_copy.wait_recv()
    cot_full = jnp.concatenate(
        [cotf[0].reshape(cells, C), cotf[1].reshape(cells, C)], axis=1
    )

    for k in range(K):
        part = dot(cot_full, weight[k], 1, 1).astype(BF)
        spread[:, J * k : J * k + J] = part.reshape(R, J, C)

    def back(i, _):
        part = dot(tiles[i], spread[i], 0, 0)
        acc[pl.ds(i, 8)] += part.reshape(8, QS, C)
        return _

    for side in (0, 1):
        recv_wait(ein.at[side], r_f.at[side])
        cols = ein[side].astype(F32)
        at = 8 - lon_half if side == 0 else 8 + J
        for r in range(R):
            ext[r + half, at : at + lon_half] = cols[4 * r : 4 * r + 4]
    for down, has in ((0, has_up), (1, has_down)):
        first = half + R if down else 0

        @pl.when(has)
        def _():
            recv_wait(elat.at[down], r_f.at[6 + down])
            for r in range(half):
                ext[first + r, 8 : 8 + J] = elat[down, r].astype(F32)
            for side in (0, 1):
                recv_wait(ecorn.at[2 * side + down], r_f.at[2 + 2 * side + down])
                cols = ecorn[2 * side + down].astype(F32)
                at = 8 - lon_half if side == 0 else 8 + J
                skip = 0 if down else 4
                for r in range(half):
                    ext[first + r, at : at + lon_half] = cols[skip + 4 * r : skip + 4 * r + 4]

    extb[...] = ext[...].astype(BF)

    def mix(i, _):
        window = extb[pl.ds(i, 8)].reshape(8 * QS, C)
        row = dot(tiles[i], window, 1, 0).astype(BF)
        for k in range(K):
            mixed[k, pl.ds(pl.multiple_of(i * J, J), J)] = row[J * k : J * k + J]
        return _

    lax.fori_loop(0, R, mix, 0, unroll=8)

    start_k = (lats + [l])[0] * per_lat // C

    def grad(step):
        k = lax.rem(start_k + step, K)
        g = dot(mixed[k], cot_full, 0, 0)
        at = pl.ds(pl.multiple_of(k * C, C), C)
        gf[at] = g
        gb[at] = g.astype(BF)

    head = -(-per_lat // C) + (0 if per_lat % C == 0 or L == 2 else 1)
    for step in range(head):
        grad(step)

    cut = -(-pc // 32) * 16
    pieces = [(0, cut), (cut, pc - cut)] if pc > cut else [(0, pc)]

    def part(p):
        return pl.ds(pieces[p][0], pieces[p][1])

    def rows(lat, c, p):
        start = lat * per_lat + jnp.minimum(c * pc, per_lat - pc) + pieces[p][0]
        return pl.ds(pl.multiple_of(start, 16), pieces[p][1])

    P2 = range(len(pieces))

    order = lons + [n]

    def rx_copy(lat, c, p):
        return remote(
            gb.at[rows(lat, c, p)], rx.at[l, c, part(p)], s_rx.at[lat, c, p], r_rx.at[l, c, p], dev(lat, n)
        )

    for c in order:
        for lat in lats[:1]:
            for p in P2:
                rx_copy(lat, c, p).start()
    for step in range(head, K):
        grad(step)
    for c in order:
        for lat in lats[1:]:
            for p in P2:
                rx_copy(lat, c, p).start()

    def rz_copy(c, p):
        return remote(zb.at[c, part(p)], rz.at[n, part(p)], s_rz.at[c, p], r_rz.at[n, p], dev(l, c))

    def lat_sum(c, p):
        total = gf[rows(l, c, p)]
        for lat in lats:
            recv_wait(rx.at[lat, c, part(p)], r_rx.at[lat, c, p])
            total = total + rx[lat, c, part(p)].astype(F32)
        return total

    def pass_on(c):
        for p in P2:
            zb[c, part(p)] = lat_sum(c, p).astype(BF)
            rz_copy(c, p).start()

    total = dot(mixed[0], weight[0], 1, 0)
    for k in range(1, K):
        total = total + dot(mixed[k], weight[k], 1, 0)
    pout[0] = total[:, :C]
    pout[1] = total[:, C:]
    out_copy = remote(pout.at[1 - ch], pin, s_ch.at[1], r_ch.at[1], mate)
    out_copy.start()

    lax.fori_loop(0, R, back, 0, unroll=8)

    gpk[...] = jnp.zeros_like(gpk)
    for side in (0, 1):
        at = 8 - lon_half if side == 0 else 8 + J
        for r in range(R):
            gpk[side, 4 * r : 4 * r + 4] = acc[r + half, at : at + lon_half]
        for r in range(half):
            gpk[side, 64 + 4 * r : 68 + 4 * r] = acc[r, at : at + lon_half]
            gpk[side, 80 + 4 * r : 84 + 4 * r] = acc[R + half + r, at : at + lon_half]
    gedge[...] = gpk[...].astype(BF)
    bwd = edge_copies(
        lambda s: gedge.at[s, pl.ds(0, 64)],
        lambda s: gin.at[s],
        lambda s, d: gedge.at[s, pl.ds(80 if d else 64, 16)],
        lambda s, d: gcorn.at[2 * s + d],
        lambda d: acc.at[pl.ds(R + half if d else 0, half), pl.ds(8, J)],
        lambda d: glat.at[d],
        s_g,
        r_g,
    )
    each(bwd, lambda c: c.start())

    for c in lons:
        pass_on(c)
    for p in P2:
        zown[part(p)] = lat_sum(n, p)

    def az_copy(lon, p):
        here = wg.at[l, n, part(p)]
        return remote(here, here, s_az.at[lon, p], r_az.at[n, p], dev(l, lon))

    def ax_copy(lat, c, p):
        return remote(
            wg.at[l, c, part(p)], wg_hbm.at[l, c, part(p)], s_ax.at[lat, c, p], r_ax.at[l, c, p], dev(lat, n)
        )

    for p in P2:
        total = zown[part(p)]
        for c in lons[::-1]:
            recv_wait(rz.at[c, part(p)], r_rz.at[c, p])
            total = total + rz[c, part(p)].astype(F32)
        wg[l, n, part(p)] = total.astype(BF)
        for lon in lons:
            az_copy(lon, p).start()
        for lat in lats:
            ax_copy(lat, n, p).start()

    out_copy.wait_recv()
    out[...] = (pout[ch] + pin[...]).astype(BF).reshape(R, J, C)
    results = [pltpu.make_async_copy(out, out_hbm, s_out.at[0])]
    results[-1].start()

    for side in (0, 1):
        recv_wait(gin.at[side], r_g.at[side])
        cols = gin[side].astype(F32)
        at = 8 if side == 0 else 8 + J - lon_half
        for r in range(R):
            acc[r + half, at : at + lon_half] += cols[4 * r : 4 * r + 4]
    for down, has in ((0, has_up), (1, has_down)):
        first = R if down else half

        @pl.when(has)
        def _():
            recv_wait(glat.at[down], r_g.at[6 + down])
            for r in range(half):
                acc[first + r, 8 : 8 + J] += glat[down, r]
            for side in (0, 1):
                recv_wait(gcorn.at[2 * side + down], r_g.at[2 + 2 * side + down])
                cols = gcorn[2 * side + down].astype(F32)
                at = 8 if side == 0 else 8 + J - lon_half
                for r in range(half):
                    acc[first + r, at : at + lon_half] += cols[4 * r : 4 * r + 4]
    for r in range(R):
        igrad[r] = acc[r + half, 8 : 8 + J].astype(BF)
    results.append(pltpu.make_async_copy(igrad, igrad_hbm, s_out.at[1]))
    results[-1].start()

    def chunk_out(lat, c, at):
        results.append(pltpu.make_async_copy(wg.at[lat, c], wg_hbm.at[lat, c], s_out.at[at]))
        results[-1].start()

    chunk_out(l, n, 2)

    near = lons[::-1]
    for i, c in enumerate(near):
        for p in P2:
            recv_wait(wg.at[l, c, part(p)], r_az.at[c, p])
            for lat in lats:
                ax_copy(lat, c, p).start()
        chunk_out(l, c, 3 + i)
    for c in [n] + near:
        for lat in lats:
            for p in P2:
                recv_wait(wg_hbm.at[lat, c, part(p)], r_ax.at[lat, c, p])

    for result in results:
        result.wait()
    cot_copy.wait_send()
    out_copy.wait_send()
    each(fwd, lambda c: c.wait_send())
    each(bwd, lambda c: c.wait_send())
    for c in lons:
        for p in P2:
            rz_copy(c, p).wait_send()
            az_copy(c, p).wait_send()
    for c in order:
        for lat in lats:
            for p in P2:
                rx_copy(lat, c, p).wait_send()
                ax_copy(lat, c, p).wait_send()


def body(features, basis, active, reach, weight, cotangent):
    R, J, C = features.shape
    K, rows, lat_span, lon_span = basis.shape
    half, lon_half = (lat_span - 1) // 2, (lon_span - 1) // 2
    O = weight.shape[2]
    L, N = lax.axis_size("lat"), lax.axis_size("lon")
    per_lat = K * C // L
    pc = -(-per_lat // (16 * N)) * 16
    cells = R * J

    dma = pltpu.SemaphoreType.DMA
    output, input_grad, wg = pl.pallas_call(
        functools.partial(kernel, (L, N, half, lon_half, per_lat, pc)),
        out_shape=(
            jax.ShapeDtypeStruct((R, J, C), BF),
            jax.ShapeDtypeStruct((R, J, C), BF),
            jax.ShapeDtypeStruct((L, N, pc, O), BF),
        ),
        in_specs=[pl.BlockSpec(memory_space=pltpu.HBM)] * 6,
        out_specs=(pl.BlockSpec(memory_space=pltpu.HBM),) * 3,
        scratch_shapes=[
            pltpu.VMEM((R, J, C), BF),
            pltpu.VMEM((R, J, C), BF),
            pltpu.VMEM((L, N, pc, O), BF),
            dma((2 + N,)),
            pltpu.VMEM((R, J, C), BF),
            pltpu.VMEM((K, lon_span, lat_span, rows), BF),
            pltpu.VMEM((lat_span, rows), jnp.int32),
            pltpu.VMEM((1, rows), jnp.int32),
            pltpu.VMEM((K, C, O), BF),
            pltpu.VMEM((R, J, C), BF),
            dma((6,)),
            pltpu.VMEM((K, rows, 8 * QS), F32),
            pltpu.VMEM((R + 8, QS, C), F32),
            pltpu.VMEM((R + 8, QS, C), BF),
            pltpu.VMEM((R + 8, QS, C), F32),
            pltpu.VMEM((R, K * J, 8 * QS), BF),
            pltpu.VMEM((K, cells, C), BF),
            pltpu.VMEM((R, K * J, C), BF),
            pltpu.VMEM((2, R, J, C), BF),
            pltpu.VMEM((2, cells, C), F32),
            pltpu.VMEM((cells, C), F32),
            pltpu.VMEM((2, 64, C), F32),
            pltpu.VMEM((2, 64, C), BF),
            pltpu.VMEM((2, 64, C), BF),
            pltpu.VMEM((4, 16, C), BF),
            pltpu.VMEM((2, half, J, C), BF),
            pltpu.VMEM((2, 96, C), F32),
            pltpu.VMEM((2, 96, C), BF),
            pltpu.VMEM((2, 64, C), BF),
            pltpu.VMEM((4, 16, C), BF),
            pltpu.VMEM((2, half, J, C), F32),
            pltpu.VMEM((K * C, O), F32),
            pltpu.VMEM((K * C, O), BF),
            pltpu.VMEM((L, N, pc, O), BF),
            pltpu.VMEM((N, pc, O), BF),
            pltpu.VMEM((N, pc, O), BF),
            pltpu.VMEM((pc, O), F32),
            dma((2,)),
            dma((2,)),
            dma((8,)),
            dma((8,)),
            dma((8,)),
            dma((8,)),
            dma((L, N, 2)),
            dma((L, N, 2)),
            dma((N, 2)),
            dma((N, 2)),
            dma((N, 2)),
            dma((N, 2)),
            dma((L, N, 2)),
            dma((L, N, 2)),
        ],
        compiler_params=pltpu.CompilerParams(
            collective_id=0, has_side_effects=True, vmem_limit_bytes=GRANT
        ),
    )(
        features,
        basis.transpose(0, 3, 2, 1),
        active.T,
        reach.reshape(1, -1),
        weight,
        cotangent,
    )
    weight_grad = wg.reshape(L, N * pc, O)[:, :per_lat].reshape(K, C, O).astype(F32)
    return output, input_grad, weight_grad


def solution(mesh):
    return jax.shard_map(
        body,
        mesh=mesh,
        in_specs=(
            P(("ens", "lat"), "lon", "ch"),
            P(),
            P(),
            P(),
            P(None, "ch", None),
            P(("ens", "lat"), "lon", "ch"),
        ),
        out_specs=(
            P(("ens", "lat"), "lon", "ch"),
            P(("ens", "lat"), "lon", "ch"),
            P("ens", "ch", None),
        ),
        check_vma=False,
    )
```
